32 devices in a mesh: orb: 16 (over z, x, core), grp: 2 (over y).
Axes of the slice: x: 2, y: 2, z: 4, core: 2. Of those that a mesh axis runs over, the one named last changes fastest.
Arguments:
- orbitals: float32 [512, 32, 1024], P('orb', 'grp'), may hold values from -6 to 6
- anchors: int32 [512], replicated, may hold values from 0 to 8
- wanted: int32 [16, 16, 2], replicated, may hold values from -1 to 511, as said below
- pairs: int32 [16, 2, 240, 2], P('orb'), may hold values from 0 to 511, as said below
- counts: int32 [16, 2], P('orb'), may hold values from 1 to 240, as said below
Outputs:
- exchange_field: float32 [512, 32, 1024], P('orb', 'grp')
The draws below stay inside these ranges and needn't reach their ends.
Inputs may be any that keep to these rules, and one draw needn't show every extreme that they name: wanted[r, o] lists up to 2 different orbitals owned by group o (ids o * 32 to o * 32 + 31), -1 in empty slots; wanted[r, r] is empty; in every draw some pairs (r, o) fill all 2 slots. pairs[r, g, p] = (i, c) with i owned by group r and c below 64; a code below 32 never names i itself; pairs may repeat. `counts`: in each group r, one device g holds exactly 240 live pairs.
All inputs are finite; a program needn't handle non-finite values.
Results may differ from the reference program's by a relative error of at most 0.0085.
Values may be sent and summed in bfloat16 or wider, within the bound.
A program may use at most 128 MiB of HBM per device.

```python
import math
import jax
import jax.numpy as jnp
from jax import lax

BOX = 32
SHIFT = 8
ORB_DEV = 32
CAP = 240
SLOT = 2
ORBITALS = 512
N_ORB = 16
N_GRP = 2


def draw_orbitals(key, part):
    streams = jax.random.split(jax.random.fold_in(key, 37), 1)
    noise = jax.random.normal(streams[0], (ORBITALS, BOX, BOX * BOX), jnp.float32)
    values = noise
    return jnp.clip(values, -6.0, 6.0)


def make_lists(key):
    streams = jax.random.split(jax.random.fold_in(key, 29), 6)
    asking = jnp.arange(N_ORB, dtype=jnp.int32)[:, None, None]
    owning = jnp.arange(N_ORB, dtype=jnp.int32)[None, :, None]
    coin_flip = jax.random.randint(streams[0], (N_ORB, N_ORB, SLOT), 0, 2)
    forced = owning == (asking + 1) % N_ORB
    is_live = ((coin_flip == 1) | forced) & (owning != asking)
    scores = jax.random.randint(streams[1], (N_ORB, N_ORB, ORB_DEV), 0, 1 << 20) * ORB_DEV + jnp.arange(ORB_DEV, dtype=jnp.int32)
    chosen = jnp.argsort(scores, axis=-1)[..., :SLOT].astype(jnp.int32)
    wanted = jnp.where(is_live, owning * ORB_DEV + chosen, -1).astype(jnp.int32)
    flat_rows = wanted.reshape(N_ORB, N_ORB * SLOT)
    alive = (flat_rows >= 0).astype(jnp.int32)
    number = jnp.sum(alive, axis=1)
    ordinal = jnp.cumsum(alive, axis=1) - 1
    extent = (N_ORB, N_GRP, CAP)
    group_ids = jnp.arange(N_ORB, dtype=jnp.int32)[:, None, None]
    first_local = jax.random.randint(streams[2], extent, 0, ORB_DEV)
    stride = jax.random.randint(streams[3], extent, 1, ORB_DEV)
    own_code = (first_local + stride) % ORB_DEV
    picked = jax.random.randint(streams[4], extent, 0, 1 << 20) % number[:, None, None]
    matches = (ordinal[:, None, None, :] == picked[..., None]) & (alive[:, None, None, :] == 1)
    positions = jnp.arange(N_ORB * SLOT, dtype=jnp.int32)
    far_code = ORB_DEV + jnp.sum(jnp.where(matches, positions, 0), axis=-1)
    side_flip = jax.random.randint(streams[5], extent, 0, 2)
    second_code = jnp.where(side_flip == 0, own_code, far_code)
    first_ids = group_ids * ORB_DEV + first_local
    pairs = jnp.stack([first_ids, second_code], axis=-1).astype(jnp.int32)
    return (wanted, pairs)


def draw_wanted(key, part):
    return make_lists(key)[0]


def draw_pairs(key, part):
    return make_lists(key)[1]


def draw_counts(key, part):
    streams = jax.random.split(jax.random.fold_in(key, 31), 2)
    heaviest = jax.random.randint(streams[0], (N_ORB, 1), 0, N_GRP)
    lighter = jax.random.randint(streams[1], (N_ORB, N_GRP), max(1, CAP // 8), CAP // 3 + 1)
    return jnp.where(jnp.arange(N_GRP, dtype=jnp.int32)[None, :] == heaviest, CAP, lighter).astype(jnp.int32)


def plant(result, own_key, low, top_value):
    shape = result.shape
    index_at = [jax.random.randint(jax.random.fold_in(own_key, axis), (), 0, shape[axis]) for axis in range(len(shape))]
    result = result.at[tuple(index_at)].set(low)
    longest = shape.index(max(shape))
    index_at[longest] = (index_at[longest] + 1) % shape[longest]
    return result.at[tuple(index_at)].set(top_value)


def setup_inputs(seed: int = 0) -> dict:
    key_of = jax.random.split(jax.random.key(seed), 6)
    return {
        "orbitals": draw_orbitals(jax.random.fold_in(key_of[5], 71), 0),
        "anchors": plant(jax.random.randint(key_of[1], (ORBITALS,), 0, SHIFT + 1), jax.random.fold_in(key_of[1], 1), 0, SHIFT).astype(jnp.int32),
        "wanted": draw_wanted(jax.random.fold_in(key_of[5], 71), 0),
        "pairs": draw_pairs(jax.random.fold_in(key_of[5], 71), 0),
        "counts": draw_counts(jax.random.fold_in(key_of[5], 71), 0),
    }


screening = 0.01
block_pairs = 16

def sine_table(extent):
    ordinal = jnp.arange(extent, dtype=jnp.float32) + 1.0
    angles = math.pi * ordinal[:, None] * ordinal[None, :] / (extent + 1)
    return (math.sqrt(2.0 / (extent + 1)) * jnp.sin(angles)).astype(jnp.bfloat16)

def denominator(extent):
    ordinal = jnp.arange(extent, dtype=jnp.float32) + 1.0
    eigenvalue = 4.0 * jnp.sin(math.pi * ordinal / (2 * (extent + 1))) ** 2
    return eigenvalue[:, None, None] + eigenvalue[None, :, None] + eigenvalue[None, None, :] + screening

def displaced(box_batch, offset):
    margin = box_batch.shape[1] // 4
    padded = jnp.pad(box_batch, ((0, 0), (margin, margin), (0, 0)))

    def single(source, start_row):
        return lax.dynamic_slice_in_dim(source, start_row, box_batch.shape[1], 0)
    return jax.vmap(single)(padded, (margin - offset).astype(jnp.int32))

def potential(density, sine_rows, divisor):
    sine_wide = sine_rows.astype(jnp.float32)

    def along(values, form):
        return jnp.einsum(form, sine_wide, values.astype(jnp.float32), precision=lax.Precision.HIGHEST)
    section_one = along(density, 'kx,pxyz->pkyz').astype(jnp.bfloat16)
    section_two = along(section_one, 'kz,pxyz->pxyk').astype(jnp.bfloat16)
    section_three = (along(section_two, 'ky,pxyz->pxkz') / divisor).astype(jnp.bfloat16)
    section_four = along(section_three, 'ky,pxyz->pxkz').astype(jnp.bfloat16)
    section_five = along(section_four, 'kz,pxyz->pxyk').astype(jnp.bfloat16)
    return along(section_five, 'kx,pxyz->pkyz').astype(jnp.bfloat16)

def pair_terms(first_boxes, second_boxes, offset, sine_rows, divisor):
    batch_size, extent, plane_size = first_boxes.shape
    shifted_box = displaced(second_boxes, offset)
    density = (first_boxes.astype(jnp.float32) * shifted_box.astype(jnp.float32)).astype(jnp.bfloat16)
    field_cube = potential(density.reshape(batch_size, extent, extent, extent), sine_rows, divisor)
    field_wide = field_cube.reshape(batch_size, extent, plane_size).astype(jnp.float32)
    own_term = field_wide * shifted_box.astype(jnp.float32)
    other_term = displaced(field_wide * first_boxes.astype(jnp.float32), -offset)
    return (own_term, other_term)

def reference(orbitals, anchors, wanted, pairs, counts):
    orbit_count, extent, plane_size = orbitals.shape
    group_total, group_size, capacity = (pairs.shape[0], pairs.shape[1], pairs.shape[2])
    own_count = orbit_count // group_total
    request_flat = wanted.reshape(group_total, -1).astype(jnp.int32)
    request_width = request_flat.shape[1]
    group_row = jnp.broadcast_to(jnp.arange(group_total, dtype=jnp.int32)[:, None, None], (group_total, group_size, capacity)).reshape(-1)
    raw_pairs = pairs.reshape(-1, 2).astype(jnp.int32)
    code = raw_pairs[:, 1]
    far_index = jnp.clip(code - own_count, 0, request_width - 1).astype(jnp.int32)
    far_id = request_flat[group_row, far_index]
    second_full = jnp.where(code < own_count, group_row * own_count + code, far_id).astype(jnp.int32)
    flat_pairs = jnp.stack([raw_pairs[:, 0], second_full], axis=-1).astype(jnp.int32)
    slot_total = flat_pairs.shape[0]
    is_live = (jnp.arange(capacity, dtype=jnp.int32)[None, None, :] < counts[:, :, None]).reshape(-1)
    is_live = is_live & (second_full >= 0)
    ranking = (jnp.cumsum(is_live.astype(jnp.int32)) - 1).astype(jnp.int32)
    live_total = jnp.sum(is_live.astype(jnp.int32))
    target = jnp.where(is_live, ranking, slot_total + block_pairs).astype(jnp.int32)
    listed = jnp.zeros((slot_total + block_pairs, 2), jnp.int32).at[target].set(flat_pairs, mode='drop')
    boxes = orbitals.astype(jnp.bfloat16)
    sine_rows = sine_table(extent)
    divisor = denominator(extent)

    def turn(turn_index, running):
        start_row = (turn_index * block_pairs).astype(jnp.int32)
        window = lax.dynamic_slice_in_dim(listed, start_row, block_pairs, 0)
        first_ids = window[:, 0]
        second_ids = window[:, 1]
        in_range = start_row + jnp.arange(block_pairs, dtype=jnp.int32) < live_total
        offset = (anchors[second_ids] - anchors[first_ids]).astype(jnp.int32)
        own_term, other_term = pair_terms(boxes[first_ids], boxes[second_ids], offset, sine_rows, divisor)
        running = running.at[jnp.where(in_range, first_ids, orbit_count)].add(own_term, mode='drop')
        running = running.at[jnp.where(in_range, second_ids, orbit_count)].add(other_term, mode='drop')
        return running
    rounds = (live_total + block_pairs - 1) // block_pairs
    initial = jnp.zeros((orbit_count, extent, plane_size), jnp.float32)
    return lax.fori_loop(0, rounds, turn, initial)
```

```python
import functools
import math

import jax
import jax.numpy as jnp
from jax import lax
from jax.experimental import pallas as pl
from jax.experimental.pallas import tpu as pltpu
from jax.sharding import PartitionSpec as P

screening = 0.01
batch = 8
lanes = 128


def sine_table(extent):
    ordinal = jnp.arange(extent, dtype=jnp.float32) + 1.0
    angles = math.pi * ordinal[:, None] * ordinal[None, :] / (extent + 1)
    return (math.sqrt(2.0 / (extent + 1)) * jnp.sin(angles)).astype(jnp.bfloat16)


def denominator(extent):
    ordinal = jnp.arange(extent, dtype=jnp.float32) + 1.0
    eigenvalue = 4.0 * jnp.sin(math.pi * ordinal / (2 * (extent + 1))) ** 2
    return (
        eigenvalue[:, None, None]
        + eigenvalue[None, :, None]
        + eigenvalue[None, None, :]
        + screening
    )


def list_kernel(sizes, where, pairs, counts, anchors, request, listed, total, spare, tally):
    group_size, capacity, own_count, per_owner, per, slots, pad = sizes
    member, position = where[0], where[1]
    dead = own_count + slots

    def pack(first, second, offset):
        return first + second * 256 + (offset + pad) * 65536

    for g in range(group_size):
        tally[g] = 0

    def scan(g, p, state):
        mine, own = state
        at = (g * capacity + p) * 2
        first_id, code = pairs[at], pairs[at + 1]
        first = jnp.clip(first_id - member * own_count, 0, own_count - 1)
        is_own = code < own_count
        slot = jnp.clip(code - own_count, 0, request.shape[0] - 1)
        second_id = jnp.where(is_own, member * own_count + code, request[slot])
        valid = second_id >= 0
        offset = anchors[jnp.maximum(second_id, 0)] - anchors[first_id]
        offset = jnp.clip(offset, -pad, pad)
        owner, sub = slot // per_owner, slot % per_owner
        if group_size <= per_owner:
            holder, local = sub // per, owner * per + sub % per
        else:
            holder, local = sub + per_owner * (owner % (group_size // per_owner)), owner

        here = jnp.logical_and(valid, jnp.logical_and(~is_own, holder == position))
        listed[mine] = pack(first, own_count + local, offset)
        spare[own] = pack(first, jnp.clip(code, 0, own_count - 1), offset)
        far = jnp.where(jnp.logical_and(valid, ~is_own), 1, 0)
        tally[holder] = tally[holder] + far
        return (
            mine + jnp.where(here, 1, 0),
            own + jnp.where(is_own, 1, 0),
        )

    state = (jnp.int32(0), jnp.int32(0))
    for g in range(group_size):
        state = lax.fori_loop(0, counts[g], functools.partial(scan, g), state)
    mine, own = state
    everything = own
    for g in range(group_size):
        everything = everything + tally[g]
    share = (everything + group_size - 1) // group_size
    begin = jnp.int32(0)
    for g in range(group_size):
        begin = begin + jnp.where(g < position, jnp.maximum(share - tally[g], 0), 0)
    stop = jnp.minimum(begin + jnp.maximum(share - mine, 0), own)
    begin = jnp.minimum(begin, own)

    def take(i, count):
        listed[count] = spare[i]
        return count + 1

    mine = lax.fori_loop(begin, stop, take, mine)
    for i in range(batch):
        listed[mine + i] = pack(dead, dead, 0)
    total[0] = mine


def pair_kernel(
    sizes, listed, total, own, far, plane, first_block, scale, own_out, far_out,
    boxes, sums, density, middle, field,
):
    own_count, slots, extent, width, pad = sizes
    chunks = width // lanes
    tall = extent + 2 * pad
    dead = own_count + slots
    inner = slice(pad, pad + extent)
    zeros = jnp.zeros((tall, lanes), jnp.float32)
    edge = jnp.zeros((pad, lanes), jnp.float32)

    def clear(n, carry):
        for s in range(chunks):
            sums[n, s] = zeros
        return carry

    lax.fori_loop(0, dead + 1, clear, 0)

    def fill(source, base, n, carry):
        for s in range(chunks):
            boxes[base + n, s, :pad] = edge
            boxes[base + n, s, inner] = source[n, :, s * lanes : (s + 1) * lanes].astype(jnp.float32)
            boxes[base + n, s, pad + extent :] = edge
        return carry

    lax.fori_loop(0, own_count, functools.partial(fill, own, 0), 0)
    lax.fori_loop(0, slots, functools.partial(fill, far, own_count), 0)
    for s in range(chunks):
        boxes[dead, s] = zeros

    def unpack(turn, b):
        word = listed[turn * batch + b]
        first, second = word % 256, (word // 256) % 256
        return first, second, 2 * pad - word // 65536

    step = 256

    def turn_body(turn, carry):
        for b in range(batch):
            first, second, start = unpack(turn, b)
            rows = slice(b * extent, (b + 1) * extent)
            for s in range(chunks):
                moved = boxes[second, s, pl.ds(start, extent), :]
                product = boxes[first, s, inner] * moved
                density[rows, s * lanes : (s + 1) * lanes] = product.astype(jnp.bfloat16)
        for n in range(width // step):
            columns = slice(n * step, (n + 1) * step)
            wave = jnp.dot(density[...], plane[:, columns], preferred_element_type=jnp.float32)
            wave = jnp.dot(
                first_block[...], wave.astype(jnp.bfloat16), preferred_element_type=jnp.float32
            )
            wave = wave.reshape(batch, extent, step) * scale[:, columns][None]
            wave = wave.reshape(batch * extent, step).astype(jnp.bfloat16)
            wave = jnp.dot(first_block[...], wave, preferred_element_type=jnp.float32)
            middle[:, columns] = wave.astype(jnp.bfloat16)
        for n in range(width // step):
            columns = slice(n * step, (n + 1) * step)
            field[:, columns] = jnp.dot(
                middle[...], plane[:, columns], preferred_element_type=jnp.float32
            )
        for b in range(batch):
            first, second, start = unpack(turn, b)
            rows = slice(b * extent, (b + 1) * extent)
            for s in range(chunks):
                moved = boxes[second, s, pl.ds(start, extent), :]
                own_box = boxes[first, s, inner]
                value = field[rows, s * lanes : (s + 1) * lanes]
                sums[first, s, inner] += value * moved
                sums[second, s, pl.ds(start, extent), :] += value * own_box
        return carry

    lax.fori_loop(0, (total[0] + batch - 1) // batch, turn_body, 0)

    def give(target, base, n, carry):
        for s in range(chunks):
            target[n, :, s * lanes : (s + 1) * lanes] = sums[base + n, s, inner].astype(target.dtype)
        return carry

    lax.fori_loop(0, own_count, functools.partial(give, own_out, 0), 0)
    lax.fori_loop(0, slots, functools.partial(give, far_out, own_count), 0)


def join_kernel(local, own, returned, out, total):
    total[...] = own[...]

    def add(n, carry):
        total[local[n]] += returned[n].astype(jnp.float32)
        return carry

    lax.fori_loop(0, returned.shape[0], add, 0)
    out[...] = total[...].astype(out.dtype)


def shards(orbitals, anchors, wanted, pairs, counts):
    group_size = lax.axis_size("grp")
    member = lax.axis_index("orb")
    position = lax.axis_index("grp")
    own_count = orbitals.shape[0]
    extent = orbitals.shape[1] * group_size
    width = orbitals.shape[2]
    pad = extent // 4
    owners, per_owner = wanted.shape[0], wanted.shape[2]
    per = -(-per_owner // group_size)
    slots = owners * per
    capacity = pairs.shape[2]
    smem = pl.BlockSpec(memory_space=pltpu.SMEM)
    vmem = pl.BlockSpec(memory_space=pltpu.VMEM)

    own_full = lax.all_gather(orbitals.astype(jnp.bfloat16), "grp", axis=1, tiled=True)

    sine_rows = sine_table(extent)
    plane = jnp.kron(sine_rows, sine_rows)
    first_block = jnp.kron(jnp.eye(batch, dtype=jnp.bfloat16), sine_rows)
    scale = (1.0 / denominator(extent)).reshape(extent, width)

    send_ids = lax.dynamic_index_in_dim(wanted, member, 1, keepdims=False)
    request = lax.dynamic_index_in_dim(wanted, member, 0, keepdims=False).reshape(-1)
    if group_size <= per_owner:
        send_ids = jnp.pad(send_ids, ((0, 0), (0, per * group_size - per_owner)), constant_values=-1)
        start = position * per
    else:
        start = position % per_owner
    send_ids = lax.dynamic_slice_in_dim(send_ids, start, per, 1).reshape(slots)
    send_local = jnp.where(send_ids >= 0, send_ids - member * own_count, 0)

    size = group_size * capacity + 2 * batch
    sizes = (group_size, capacity, own_count, per_owner, per, slots, pad)
    listed, total = pl.pallas_call(
        functools.partial(list_kernel, sizes),
        out_shape=(
            jax.ShapeDtypeStruct((size,), jnp.int32),
            jax.ShapeDtypeStruct((1,), jnp.int32),
        ),
        in_specs=[smem] * 5,
        out_specs=(smem, smem),
        scratch_shapes=[pltpu.SMEM((size,), jnp.int32), pltpu.SMEM((group_size,), jnp.int32)],
    )(
        jnp.stack([member, position]).astype(jnp.int32),
        pairs.reshape(-1),
        counts.reshape(-1),
        anchors,
        request,
    )

    far_full = lax.all_to_all(own_full[send_local], "orb", split_axis=0, concat_axis=0, tiled=True)

    tall = extent + 2 * pad
    chunks = width // lanes
    kept = own_count + slots + 1
    own_sum, far_sum = pl.pallas_call(
        functools.partial(pair_kernel, (own_count, slots, extent, width, pad)),
        out_shape=(
            jax.ShapeDtypeStruct((own_count, extent, width), jnp.float32),
            jax.ShapeDtypeStruct((slots, extent, width), jnp.bfloat16),
        ),
        in_specs=[smem, smem] + [vmem] * 5,
        out_specs=(vmem, vmem),
        scratch_shapes=[
            pltpu.VMEM((kept, chunks, tall, lanes), jnp.float32),
            pltpu.VMEM((kept, chunks, tall, lanes), jnp.float32),
            pltpu.VMEM((batch * extent, width), jnp.bfloat16),
            pltpu.VMEM((batch * extent, width), jnp.bfloat16),
            pltpu.VMEM((batch * extent, width), jnp.float32),
        ],
        compiler_params=pltpu.CompilerParams(vmem_limit_bytes=56 * 2**20),
    )(listed, total, own_full, far_full, plane, first_block, scale)

    returned = lax.all_to_all(far_sum, "orb", split_axis=0, concat_axis=0, tiled=True)
    joined = pl.pallas_call(
        join_kernel,
        out_shape=jax.ShapeDtypeStruct((own_count, extent, width), jnp.bfloat16),
        in_specs=[smem, vmem, vmem],
        out_specs=vmem,
        scratch_shapes=[pltpu.VMEM((own_count, extent, width), jnp.float32)],
        compiler_params=pltpu.CompilerParams(vmem_limit_bytes=40 * 2**20),
    )(send_local, own_sum, returned)
    return lax.psum_scatter(joined, "grp", scatter_dimension=1, tiled=True).astype(jnp.float32)


def solution(mesh):
    return jax.shard_map(
        shards,
        mesh=mesh,
        in_specs=(P("orb", "grp", None), P(), P(), P("orb", None, None, None), P("orb", None)),
        out_specs=P("orb", "grp", None),
        check_vma=False,
    )
```

```python
import functools
import math

import jax
import jax.numpy as jnp
from jax import lax
from jax.experimental import pallas as pl
from jax.experimental.pallas import tpu as pltpu
from jax.sharding import PartitionSpec as P

screening = 0.01
batch = 8
lanes = 128


def sine_table(extent):
    ordinal = jnp.arange(extent, dtype=jnp.float32) + 1.0
    angles = math.pi * ordinal[:, None] * ordinal[None, :] / (extent + 1)
    return (math.sqrt(2.0 / (extent + 1)) * jnp.sin(angles)).astype(jnp.bfloat16)


def denominator(extent):
    ordinal = jnp.arange(extent, dtype=jnp.float32) + 1.0
    eigenvalue = 4.0 * jnp.sin(math.pi * ordinal / (2 * (extent + 1))) ** 2
    return (
        eigenvalue[:, None, None]
        + eigenvalue[None, :, None]
        + eigenvalue[None, None, :]
        + screening
    )


def list_kernel(
    sizes, where, pairs, counts, anchors, request, far_list, own_list, totals, spare, tally
):
    group_size, capacity, own_count, per_owner, per, slots, pad = sizes
    member, position = where[0], where[1]

    def pack(first, second, offset):
        return first + second * 256 + (offset + pad) * 65536

    for g in range(group_size):
        tally[g] = 0

    def scan(g, p, state):
        mine, own = state
        at = (g * capacity + p) * 2
        first_id, code = pairs[at], pairs[at + 1]
        first = jnp.clip(first_id - member * own_count, 0, own_count - 1)
        is_own = code < own_count
        slot = jnp.clip(code - own_count, 0, request.shape[0] - 1)
        second_id = jnp.where(is_own, member * own_count + code, request[slot])
        valid = second_id >= 0
        offset = anchors[jnp.maximum(second_id, 0)] - anchors[first_id]
        offset = jnp.clip(offset, -pad, pad)
        owner, sub = slot // per_owner, slot % per_owner
        if group_size <= per_owner:
            holder, local = sub // per, owner * per + sub % per
        else:
            holder, local = sub + per_owner * (owner % (group_size // per_owner)), owner
        here = jnp.logical_and(valid, jnp.logical_and(~is_own, holder == position))
        far_list[mine] = pack(first, local, offset)
        spare[own] = pack(first, jnp.clip(code, 0, own_count - 1), offset)
        tally[holder] = tally[holder] + jnp.where(jnp.logical_and(valid, ~is_own), 1, 0)
        return mine + jnp.where(here, 1, 0), own + jnp.where(is_own, 1, 0)

    state = (jnp.int32(0), jnp.int32(0))
    for g in range(group_size):
        state = lax.fori_loop(0, counts[g], functools.partial(scan, g), state)
    mine, own = state
    everything = own
    for g in range(group_size):
        everything = everything + tally[g]
    share = (everything + group_size - 1) // group_size
    begin = jnp.int32(0)
    for g in range(group_size):
        begin = begin + jnp.where(g < position, jnp.maximum(share - tally[g], 0), 0)
    stop = jnp.minimum(begin + jnp.maximum(share - mine, 0), own)
    begin = jnp.minimum(begin, own)

    def take(i, carry):
        own_list[i - begin] = spare[i]
        return carry

    lax.fori_loop(begin, stop, take, 0)
    for i in range(batch):
        far_list[mine + i] = pack(own_count, slots, 0)
        own_list[stop - begin + i] = pack(own_count, own_count, 0)
    totals[0] = mine
    totals[1] = stop - begin


def pair_kernel(
    far, own_count, extent, width, pad, listed, totals, own_full, other, plane, first_block,
    scale, *rest,
):
    if far:
        own_out, far_out, firsts, seconds, first_sums, second_sums, density, middle, field = rest
    else:
        own_out, firsts, seconds, first_sums, second_sums, density, middle, field = rest
    chunks = width // lanes
    tall = extent + 2 * pad
    second_count = seconds.shape[0] - 1
    inner = slice(pad, pad + extent)
    zeros = jnp.zeros((chunks, tall, lanes), jnp.float32)
    edge = jnp.zeros((chunks, pad, lanes), jnp.float32)

    def part(s):
        return slice(s * lanes, (s + 1) * lanes)

    def fill_own(n, carry):
        for s in range(chunks):
            box = own_full[n, :, part(s)].astype(jnp.float32)
            firsts[n, s] = box
            if far:
                first_sums[n, s] = jnp.zeros_like(box)
            else:
                seconds[n, s, inner] = box
                first_sums[n, s] = other[n, :, part(s)]
        return carry

    def fill_far(n, carry):
        group_size, per, rows = other.shape[1:4]
        for h in range(group_size):
            for s in range(chunks):
                seconds[n, s, pad + h * rows : pad + (h + 1) * rows] = other[
                    n // per, h, n % per, :, part(s)
                ].astype(jnp.float32)
        return carry

    def clear(n, carry):
        seconds[n, :, :pad] = edge
        seconds[n, :, pad + extent :] = edge
        second_sums[n] = zeros
        return carry

    lax.fori_loop(0, second_count, clear, 0)
    lax.fori_loop(0, own_count, fill_own, 0)
    if far:
        lax.fori_loop(0, second_count, fill_far, 0)
    firsts[own_count] = jnp.zeros((chunks, extent, lanes), jnp.float32)
    first_sums[own_count] = jnp.zeros((chunks, extent, lanes), jnp.float32)
    seconds[second_count] = zeros
    second_sums[second_count] = zeros

    def unpack(turn, b):
        word = listed[turn * batch + b]
        return word % 256, (word // 256) % 256, 2 * pad - word // 65536

    step = 256
    some = 4 if chunks % 4 == 0 else 1

    def turn_body(turn, carry):
        for b in range(batch):
            first, second, start = unpack(turn, b)
            rows = slice(b * extent, (b + 1) * extent)
            for s in range(chunks):
                moved = seconds[second, s, pl.ds(start, extent), :]
                density[rows, part(s)] = (firsts[first, s] * moved).astype(jnp.bfloat16)
        for n in range(width // step):
            columns = slice(n * step, (n + 1) * step)
            wave = jnp.dot(density[...], plane[:, columns], preferred_element_type=jnp.float32)
            wave = jnp.dot(
                first_block[...], wave.astype(jnp.bfloat16), preferred_element_type=jnp.float32
            )
            wave = wave.reshape(batch, extent, step) * scale[:, columns][None]
            wave = wave.reshape(batch * extent, step).astype(jnp.bfloat16)
            wave = jnp.dot(first_block[...], wave, preferred_element_type=jnp.float32)
            middle[:, columns] = wave.astype(jnp.bfloat16)
        for n in range(width // step):
            columns = slice(n * step, (n + 1) * step)
            field[:, columns] = jnp.dot(
                middle[...], plane[:, columns], preferred_element_type=jnp.float32
            )
        for b in range(batch):
            first, second, start = unpack(turn, b)
            rows = slice(b * extent, (b + 1) * extent)
            window = pl.ds(start, extent)
            for q in range(0, chunks, some):
                group = range(q, q + some)
                firsts_were = [first_sums[first, s] for s in group]
                seconds_were = [second_sums[second, s, window, :] for s in group]
                values = [field[rows, part(s)] for s in group]
                for k, s in enumerate(group):
                    first_sums[first, s] = (
                        firsts_were[k] + values[k] * seconds[second, s, window, :]
                    )
                for k, s in enumerate(group):
                    second_sums[second, s, window, :] = (
                        seconds_were[k] + values[k] * firsts[first, s]
                    )
        return carry

    lax.fori_loop(0, (totals[0 if far else 1] + batch - 1) // batch, turn_body, 0)

    def give_own(n, carry):
        for s in range(chunks):
            value = first_sums[n, s]
            if not far:
                value = value + second_sums[n, s, inner]
            own_out[n, :, part(s)] = value.astype(own_out.dtype)
        return carry

    def give_far(n, carry):
        group_size, per, rows = far_out.shape[1:4]
        for h in range(group_size):
            for s in range(chunks):
                far_out[n // per, h, n % per, :, part(s)] = second_sums[
                    n, s, pad + h * rows : pad + (h + 1) * rows
                ].astype(far_out.dtype)
        return carry

    lax.fori_loop(0, own_count, give_own, 0)
    if far:
        lax.fori_loop(0, second_count, give_far, 0)


def join_kernel(local, own, returned, out):
    out[...] = own[...].astype(jnp.float32)

    def add(n, carry):
        out[local[n]] += returned[n].astype(jnp.float32)
        return carry

    lax.fori_loop(0, returned.shape[0], add, 0)


def shards(orbitals, anchors, wanted, pairs, counts):
    group_size = lax.axis_size("grp")
    member = lax.axis_index("orb")
    position = lax.axis_index("grp")
    own_count, rows, width = orbitals.shape
    extent = rows * group_size
    pad = extent // 4
    owners, per_owner = wanted.shape[0], wanted.shape[2]
    per = -(-per_owner // group_size)
    slots = owners * per
    capacity = pairs.shape[2]
    smem = pl.BlockSpec(memory_space=pltpu.SMEM)
    vmem = pl.BlockSpec(memory_space=pltpu.VMEM)

    slab = orbitals.astype(jnp.bfloat16)
    own_full = lax.all_gather(slab, "grp", axis=1, tiled=True)

    send_ids = lax.dynamic_index_in_dim(wanted, member, 1, keepdims=False)
    request = lax.dynamic_index_in_dim(wanted, member, 0, keepdims=False).reshape(-1)
    if group_size <= per_owner:
        room = per * group_size - per_owner
        send_ids = jnp.pad(send_ids, ((0, 0), (0, room)), constant_values=-1)
    else:
        send_ids = jnp.tile(send_ids, (1, -(-group_size // per_owner)))[:, :group_size]
    send_ids = send_ids.reshape(-1)
    send_local = jnp.where(send_ids >= 0, send_ids - member * own_count, 0)
    outgoing = slab[send_local]
    arrived = lax.all_to_all(outgoing, ("orb", "grp"), split_axis=0, concat_axis=0, tiled=True)
    arrived = arrived.reshape(owners, group_size, per, rows, width)

    sine_rows = sine_table(extent)
    plane = jnp.kron(sine_rows, sine_rows)
    first_block = jnp.kron(jnp.eye(batch, dtype=jnp.bfloat16), sine_rows)
    scale = (1.0 / denominator(extent)).reshape(extent, width)

    size = group_size * capacity + 2 * batch
    sizes = (group_size, capacity, own_count, per_owner, per, slots, pad)
    words = jax.ShapeDtypeStruct((size,), jnp.int32)
    far_list, own_list, totals = pl.pallas_call(
        functools.partial(list_kernel, sizes),
        out_shape=(words, words, jax.ShapeDtypeStruct((2,), jnp.int32)),
        in_specs=[smem] * 5,
        out_specs=(smem, smem, smem),
        scratch_shapes=[pltpu.SMEM((size,), jnp.int32), pltpu.SMEM((group_size,), jnp.int32)],
    )(
        jnp.stack([member, position]).astype(jnp.int32),
        pairs.reshape(-1),
        counts.reshape(-1),
        anchors,
        request,
    )

    tall = extent + 2 * pad
    chunks = width // lanes

    def run(far, listed, other, out_shape):
        count = slots if far else own_count
        return pl.pallas_call(
            functools.partial(pair_kernel, far, own_count, extent, width, pad),
            out_shape=out_shape,
            in_specs=[smem, smem] + [vmem] * 5,
            out_specs=(vmem,) * len(out_shape),
            scratch_shapes=[
                pltpu.VMEM((own_count + 1, chunks, extent, lanes), jnp.float32),
                pltpu.VMEM((count + 1, chunks, tall, lanes), jnp.float32),
                pltpu.VMEM((own_count + 1, chunks, extent, lanes), jnp.float32),
                pltpu.VMEM((count + 1, chunks, tall, lanes), jnp.float32),
                pltpu.VMEM((batch * extent, width), jnp.bfloat16),
                pltpu.VMEM((batch * extent, width), jnp.bfloat16),
                pltpu.VMEM((batch * extent, width), jnp.float32),
            ],
            cost_estimate=pl.CostEstimate(
                flops=60_000_000_000, bytes_accessed=16_000_000, transcendentals=0
            ),
            compiler_params=pltpu.CompilerParams(vmem_limit_bytes=52 * 2**20),
        )(listed, totals, own_full, other, plane, first_block, scale)

    whole = (own_count, extent, width)
    own_part, far_sum = run(
        True,
        far_list,
        arrived,
        (
            jax.ShapeDtypeStruct(whole, jnp.float32),
            jax.ShapeDtypeStruct(arrived.shape, jnp.bfloat16),
        ),
    )
    returned = lax.all_to_all(
        far_sum.reshape(-1, rows, width), ("orb", "grp"), split_axis=0, concat_axis=0, tiled=True
    )
    (own_sum,) = run(False, own_list, own_part, (jax.ShapeDtypeStruct(whole, jnp.bfloat16),))
    own_mine = lax.psum_scatter(own_sum, "grp", scatter_dimension=1, tiled=True)
    return pl.pallas_call(
        join_kernel,
        out_shape=jax.ShapeDtypeStruct((own_count, rows, width), jnp.float32),
        in_specs=[smem, vmem, vmem],
        out_specs=vmem,
        compiler_params=pltpu.CompilerParams(vmem_limit_bytes=40 * 2**20),
    )(send_local, own_mine, returned)


def solution(mesh):
    return jax.shard_map(
        shards,
        mesh=mesh,
        in_specs=(P("orb", "grp", None), P(), P(), P("orb", None, None, None), P("orb", None)),
        out_specs=P("orb", "grp", None),
        check_vma=False,
    )
```

```python
import functools
import math

import jax
import jax.numpy as jnp
from jax import lax
from jax.experimental import pallas as pl
from jax.experimental.pallas import tpu as pltpu
from jax.sharding import PartitionSpec as P

screening = 0.01
batch = 8
lanes = 128


def sine_table(extent):
    ordinal = jnp.arange(extent, dtype=jnp.float32) + 1.0
    angles = math.pi * ordinal[:, None] * ordinal[None, :] / (extent + 1)
    return (math.sqrt(2.0 / (extent + 1)) * jnp.sin(angles)).astype(jnp.bfloat16)


def denominator(extent):
    ordinal = jnp.arange(extent, dtype=jnp.float32) + 1.0
    eigenvalue = 4.0 * jnp.sin(math.pi * ordinal / (2 * (extent + 1))) ** 2
    return (
        eigenvalue[:, None, None]
        + eigenvalue[None, :, None]
        + eigenvalue[None, None, :]
        + screening
    )


def list_kernel(
    sizes, where, pairs, counts, anchors, request, listed, total, spare, tally
):
    group_size, capacity, own_count, per_owner, per, slots, pad = sizes
    member, position = where[0], where[1]
    dead = own_count + slots

    def pack(first, second, offset):
        return first + second * 256 + (offset + pad) * 65536

    for g in range(group_size):
        tally[g] = 0

    def scan(g, p, state):
        mine, own = state
        at = (g * capacity + p) * 2
        first_id, code = pairs[at], pairs[at + 1]
        first = jnp.clip(first_id - member * own_count, 0, own_count - 1)
        is_own = code < own_count
        slot = jnp.clip(code - own_count, 0, request.shape[0] - 1)
        second_id = jnp.where(is_own, member * own_count + code, request[slot])
        valid = second_id >= 0
        offset = anchors[jnp.maximum(second_id, 0)] - anchors[first_id]
        offset = jnp.clip(offset, -pad, pad)
        owner, sub = slot // per_owner, slot % per_owner
        if group_size <= per_owner:
            holder, local = sub // per, owner * per + sub % per
        else:
            holder, local = sub + per_owner * (owner % (group_size // per_owner)), owner
        here = jnp.logical_and(valid, jnp.logical_and(~is_own, holder == position))
        listed[batch + mine] = pack(first, own_count + local, offset)
        spare[own] = pack(first, jnp.clip(code, 0, own_count - 1), offset)
        tally[holder] = tally[holder] + jnp.where(jnp.logical_and(valid, ~is_own), 1, 0)
        return mine + jnp.where(here, 1, 0), own + jnp.where(is_own, 1, 0)

    state = (jnp.int32(0), jnp.int32(0))
    for g in range(group_size):
        state = lax.fori_loop(0, counts[g], functools.partial(scan, g), state)
    mine, own = state
    everything = own
    for g in range(group_size):
        everything = everything + tally[g]
    share = (everything + group_size - 1) // group_size
    begin = jnp.int32(0)
    for g in range(group_size):
        begin = begin + jnp.where(g < position, jnp.maximum(share - tally[g], 0), 0)
    stop = jnp.minimum(begin + jnp.maximum(share - mine, 0), own)
    begin = jnp.minimum(begin, own)

    def take(i, count):
        listed[batch + count] = spare[i]
        return count + 1

    mine = lax.fori_loop(begin, stop, take, mine)
    for i in range(batch):
        listed[i] = pack(dead, dead, 0)
    for i in range(3 * batch):
        listed[batch + mine + i] = pack(dead, dead, 0)
    total[0] = mine


def mirrored(value, extent):
    groups = lanes // extent
    place = lax.broadcasted_iota(jnp.int32, value.shape, len(value.shape) - 1) // extent
    result = value
    shifts = {}
    for g in range(groups):
        shifts.setdefault((groups - 1 - 2 * g) * extent % lanes, []).append(groups - 1 - g)
    for shift, places in shifts.items():
        turned = pltpu.roll(value, shift, len(value.shape) - 1) if shift else value
        chosen = place == places[0]
        for other in places[1:]:
            chosen = jnp.logical_or(chosen, place == other)
        result = jnp.where(chosen, turned, result)
    return result


def pair_kernel(
    own_count, extent, width, pad, listed, total, own, far, plane, back, first_block, scale,
    own_out, far_out, boxes, sums, density_a, density_b, middle, field_a, field_b,
):
    chunks = width // lanes
    half = chunks // 2
    side = width // 2
    tall = extent + 2 * pad
    dead = boxes.shape[0] - 1
    inner = slice(pad, pad + extent)
    zeros = jnp.zeros((chunks, tall, lanes), jnp.float32)
    edge = jnp.zeros((chunks, pad, lanes), jnp.float32)

    def part(s):
        return slice(s * lanes, (s + 1) * lanes)

    def put(n, at, rows, read):
        for s in range(half):
            boxes[n, s, at : at + rows] = read(part(s)).astype(jnp.float32)
            boxes[n, half + s, at : at + rows] = mirrored(
                read(part(chunks - 1 - s)).astype(jnp.float32), extent
            )

    def clear(n, carry):
        boxes[n, :, :pad] = edge
        boxes[n, :, pad + extent :] = edge
        sums[n] = zeros
        return carry

    def fill_own(n, carry):
        put(n, pad, extent, lambda columns: own[n, :, columns])
        return carry

    def fill_far(n, carry):
        group_size, per, rows = far.shape[1:4]
        for h in range(group_size):
            put(
                own_count + n, pad + h * rows, rows,
                lambda columns: far[n // per, h, n % per, :, columns],
            )
        return carry

    lax.fori_loop(0, dead, clear, 0)
    lax.fori_loop(0, own_count, fill_own, 0)
    lax.fori_loop(0, dead - own_count, fill_far, 0)
    boxes[dead] = zeros
    sums[dead] = zeros
    field_b[...] = jnp.zeros_like(field_b)

    def unpack(turn, b):
        word = listed[(turn + 1) * batch + b]
        return word % 256, (word // 256) % 256, 2 * pad - word // 65536

    def products(turn, density, b):
        first, second, start = unpack(turn, b)
        rows = slice(b * extent, (b + 1) * extent)
        window = pl.ds(start, extent)
        for s in range(half):
            low = boxes[first, s, inner] * boxes[second, s, window, :]
            high = boxes[first, half + s, inner] * boxes[second, half + s, window, :]
            density[rows, part(s)] = (low + high).astype(jnp.bfloat16)
            density[rows, part(half + s)] = (low - high).astype(jnp.bfloat16)

    def terms(turn, field, b):
        first, second, start = unpack(turn, b)
        rows = slice(b * extent, (b + 1) * extent)
        window = pl.ds(start, extent)
        some = 4
        for q in range(0, chunks, some):
            group = range(q, q + some)
            values = [field[rows, part(s)] for s in group]
            adds = [values[k] * boxes[second, s, window, :] for k, s in enumerate(group)]
            were = [sums[first, s, inner] for s in group]
            for k, s in enumerate(group):
                sums[first, s, inner] = were[k] + adds[k]
            adds = [values[k] * boxes[first, s, inner] for k, s in enumerate(group)]
            were = [sums[second, s, window, :] for s in group]
            for k, s in enumerate(group):
                sums[second, s, window, :] = were[k] + adds[k]

    step = 256

    def forward(density, h, n):
        columns = slice(n * step, (n + 1) * step)
        target = slice(h * side + n * step, h * side + (n + 1) * step)
        wave = jnp.dot(
            density[:, h * side : (h + 1) * side], plane[h, :, columns],
            preferred_element_type=jnp.float32,
        )
        wave = jnp.dot(
            first_block[...], wave.astype(jnp.bfloat16), preferred_element_type=jnp.float32
        )
        wave = wave.reshape(batch, extent, step) * scale[:, target][None]
        wave = wave.reshape(batch * extent, step).astype(jnp.bfloat16)
        wave = jnp.dot(first_block[...], wave, preferred_element_type=jnp.float32)
        middle[:, target] = wave.astype(jnp.bfloat16)

    def backward(field, n):
        columns = slice(n * step, (n + 1) * step)
        even = jnp.dot(middle[:, :side], back[0, :, columns], preferred_element_type=jnp.float32)
        odd = jnp.dot(middle[:, side:], back[1, :, columns], preferred_element_type=jnp.float32)
        field[:, columns] = even + odd
        field[:, side + n * step : side + (n + 1) * step] = even - odd

    def phase(turn, density, field, next_density, last_field):
        steps = [
            functools.partial(forward, density, h, n) for h in range(2) for n in range(side // step)
        ] + [functools.partial(backward, field, n) for n in range(side // step)]
        asides = []
        for b in range(batch):
            asides.append(functools.partial(terms, turn - 1, last_field, b))
            asides.append(functools.partial(products, turn + 1, next_density, b))
        done = 0
        for k, work in enumerate(steps):
            work()
            upto = len(asides) * (k + 1) // len(steps)
            for aside in asides[done:upto]:
                aside()
            done = upto

    for b in range(batch):
        products(0, density_a, b)

    def double_turn(i, carry):
        phase(2 * i, density_a, field_a, density_b, field_b)
        phase(2 * i + 1, density_b, field_b, density_a, field_a)
        return carry

    turns = (total[0] + 2 * batch - 1) // (2 * batch)
    lax.fori_loop(0, turns, double_turn, 0)
    for b in range(batch):
        terms(2 * turns - 1, field_b, b)

    def give_own(n, carry):
        for s in range(half):
            own_out[n, :, part(s)] = sums[n, s, inner].astype(own_out.dtype)
            own_out[n, :, part(chunks - 1 - s)] = mirrored(sums[n, half + s, inner], extent).astype(
                own_out.dtype
            )
        return carry

    def give_far(n, carry):
        group_size, per, rows = far_out.shape[1:4]
        for h in range(group_size):
            block = slice(pad + h * rows, pad + (h + 1) * rows)
            for s in range(half):
                far_out[n // per, h, n % per, :, part(s)] = sums[own_count + n, s, block].astype(
                    far_out.dtype
                )
                far_out[n // per, h, n % per, :, part(chunks - 1 - s)] = mirrored(
                    sums[own_count + n, half + s, block], extent
                ).astype(far_out.dtype)
        return carry

    lax.fori_loop(0, own_count, give_own, 0)
    lax.fori_loop(0, dead - own_count, give_far, 0)


def join_kernel(local, own, returned, out):
    out[...] = own[...].astype(jnp.float32)

    def add(n, carry):
        out[local[n]] += returned[n].astype(jnp.float32)
        return carry

    lax.fori_loop(0, returned.shape[0], add, 0)


def shards(orbitals, anchors, wanted, pairs, counts):
    group_size = lax.axis_size("grp")
    member = lax.axis_index("orb")
    position = lax.axis_index("grp")
    own_count, rows, width = orbitals.shape
    extent = rows * group_size
    pad = extent // 4
    owners, per_owner = wanted.shape[0], wanted.shape[2]
    per = -(-per_owner // group_size)
    slots = owners * per
    capacity = pairs.shape[2]
    smem = pl.BlockSpec(memory_space=pltpu.SMEM)
    vmem = pl.BlockSpec(memory_space=pltpu.VMEM)

    slab = orbitals.astype(jnp.bfloat16)
    own_full = lax.all_gather(slab, "grp", axis=1, tiled=True)

    send_ids = lax.dynamic_index_in_dim(wanted, member, 1, keepdims=False)
    request = lax.dynamic_index_in_dim(wanted, member, 0, keepdims=False).reshape(-1)
    if group_size <= per_owner:
        room = per * group_size - per_owner
        send_ids = jnp.pad(send_ids, ((0, 0), (0, room)), constant_values=-1)
    else:
        send_ids = jnp.tile(send_ids, (1, -(-group_size // per_owner)))[:, :group_size]
    send_ids = send_ids.reshape(-1)
    send_local = jnp.where(send_ids >= 0, send_ids - member * own_count, 0)
    outgoing = slab[send_local]
    arrived = lax.all_to_all(outgoing, ("orb", "grp"), split_axis=0, concat_axis=0, tiled=True)
    arrived = arrived.reshape(owners, group_size, per, rows, width)

    sine_rows = sine_table(extent)
    middle = extent // 2
    plane = jnp.stack([jnp.kron(sine_rows[:middle, k::2], sine_rows) for k in range(2)])
    back = jnp.stack([jnp.kron(sine_rows[k::2, :middle], sine_rows) for k in range(2)])
    first_block = jnp.kron(jnp.eye(batch, dtype=jnp.bfloat16), sine_rows)
    divisor = denominator(extent)
    divisor = jnp.concatenate([divisor[:, 0::2], divisor[:, 1::2]], axis=1)
    scale = (1.0 / divisor).reshape(extent, width)

    size = group_size * capacity + 5 * batch
    sizes = (group_size, capacity, own_count, per_owner, per, slots, pad)
    words = jax.ShapeDtypeStruct((size,), jnp.int32)
    listed, total = pl.pallas_call(
        functools.partial(list_kernel, sizes),
        out_shape=(words, jax.ShapeDtypeStruct((1,), jnp.int32)),
        in_specs=[smem] * 5,
        out_specs=(smem, smem),
        scratch_shapes=[pltpu.SMEM((size,), jnp.int32), pltpu.SMEM((group_size,), jnp.int32)],
    )(
        jnp.stack([member, position]).astype(jnp.int32),
        pairs.reshape(-1),
        counts.reshape(-1),
        anchors,
        request,
    )

    tall = extent + 2 * pad
    chunks = width // lanes

    kept = own_count + slots + 1
    own_sum, far_sum = pl.pallas_call(
        functools.partial(pair_kernel, own_count, extent, width, pad),
        out_shape=(
            jax.ShapeDtypeStruct((own_count, extent, width), jnp.bfloat16),
            jax.ShapeDtypeStruct(arrived.shape, jnp.bfloat16),
        ),
        in_specs=[smem, smem] + [vmem] * 6,
        out_specs=(vmem, vmem),
        scratch_shapes=[
            pltpu.VMEM((kept, chunks, tall, lanes), jnp.float32),
            pltpu.VMEM((kept, chunks, tall, lanes), jnp.float32),
            pltpu.VMEM((batch * extent, width), jnp.bfloat16),
            pltpu.VMEM((batch * extent, width), jnp.bfloat16),
            pltpu.VMEM((batch * extent, width), jnp.bfloat16),
            pltpu.VMEM((batch * extent, width), jnp.float32),
            pltpu.VMEM((batch * extent, width), jnp.float32),
        ],
        cost_estimate=pl.CostEstimate(
            flops=60_000_000_000, bytes_accessed=16_000_000, transcendentals=0
        ),
        compiler_params=pltpu.CompilerParams(vmem_limit_bytes=54 * 2**20),
    )(listed, total, own_full, arrived, plane, back, first_block, scale)
    returned = lax.all_to_all(
        far_sum.reshape(-1, rows, width), ("orb", "grp"), split_axis=0, concat_axis=0, tiled=True
    )
    own_mine = lax.psum_scatter(own_sum, "grp", scatter_dimension=1, tiled=True)
    return pl.pallas_call(
        join_kernel,
        out_shape=jax.ShapeDtypeStruct((own_count, rows, width), jnp.float32),
        in_specs=[smem, vmem, vmem],
        out_specs=vmem,
        compiler_params=pltpu.CompilerParams(vmem_limit_bytes=40 * 2**20),
    )(send_local, own_mine, returned)


def solution(mesh):
    return jax.shard_map(
        shards,
        mesh=mesh,
        in_specs=(P("orb", "grp", None), P(), P(), P("orb", None, None, None), P("orb", None)),
        out_specs=P("orb", "grp", None),
        check_vma=False,
    )
```

```python
import functools
import math

import jax
import jax.numpy as jnp
from jax import lax
from jax.experimental import pallas as pl
from jax.experimental.pallas import tpu as pltpu
from jax.sharding import PartitionSpec as P

screening = 0.01
batch = 8
lanes = 128


def sine_table(extent):
    ordinal = jnp.arange(extent, dtype=jnp.float32) + 1.0
    angles = math.pi * ordinal[:, None] * ordinal[None, :] / (extent + 1)
    return (math.sqrt(2.0 / (extent + 1)) * jnp.sin(angles)).astype(jnp.bfloat16)


def denominator(extent):
    ordinal = jnp.arange(extent, dtype=jnp.float32) + 1.0
    eigenvalue = 4.0 * jnp.sin(math.pi * ordinal / (2 * (extent + 1))) ** 2
    return (
        eigenvalue[:, None, None]
        + eigenvalue[None, :, None]
        + eigenvalue[None, None, :]
        + screening
    )


def list_kernel(
    sizes, where, pairs, counts, anchors, request, listed, total, spare, tally
):
    group_size, capacity, own_count, per_owner, per, slots, pad = sizes
    member, position = where[0], where[1]
    dead = own_count + slots

    def pack(first, second, offset):
        return first + second * 256 + (offset + pad) * 65536

    for g in range(group_size):
        tally[g] = 0

    def scan(g, p, state):
        mine, own = state
        at = (g * capacity + p) * 2
        first_id, code = pairs[at], pairs[at + 1]
        first = jnp.clip(first_id - member * own_count, 0, own_count - 1)
        is_own = code < own_count
        slot = jnp.clip(code - own_count, 0, request.shape[0] - 1)
        second_id = jnp.where(is_own, member * own_count + code, request[slot])
        valid = second_id >= 0
        offset = anchors[jnp.maximum(second_id, 0)] - anchors[first_id]
        offset = jnp.clip(offset, -pad, pad)
        owner, sub = slot // per_owner, slot % per_owner
        if group_size <= per_owner:
            holder, local = sub // per, owner * per + sub % per
        else:
            holder, local = sub + per_owner * (owner % (group_size // per_owner)), owner
        here = jnp.logical_and(valid, jnp.logical_and(~is_own, holder == position))
        listed[batch + mine] = pack(first, own_count + local, offset)
        spare[own] = pack(first, jnp.clip(code, 0, own_count - 1), offset)
        tally[holder] = tally[holder] + jnp.where(jnp.logical_and(valid, ~is_own), 1, 0)
        return mine + jnp.where(here, 1, 0), own + jnp.where(is_own, 1, 0)

    state = (jnp.int32(0), jnp.int32(0))
    for g in range(group_size):
        state = lax.fori_loop(0, counts[g], functools.partial(scan, g), state)
    mine, own = state
    everything = own
    for g in range(group_size):
        everything = everything + tally[g]
    share = (everything + group_size - 1) // group_size
    begin = jnp.int32(0)
    for g in range(group_size):
        begin = begin + jnp.where(g < position, jnp.maximum(share - tally[g], 0), 0)
    stop = jnp.minimum(begin + jnp.maximum(share - mine, 0), own)
    begin = jnp.minimum(begin, own)

    def take(i, count):
        listed[batch + count] = spare[i]
        return count + 1

    mine = lax.fori_loop(begin, stop, take, mine)
    for i in range(batch):
        listed[i] = pack(dead, dead, 0)
    for i in range(3 * batch):
        listed[batch + mine + i] = pack(dead, dead, 0)
    total[0] = mine


def mirrored(value, extent):
    groups = lanes // extent
    place = lax.broadcasted_iota(jnp.int32, value.shape, len(value.shape) - 1) // extent
    result = value
    shifts = {}
    for g in range(groups):
        shifts.setdefault((groups - 1 - 2 * g) * extent % lanes, []).append(groups - 1 - g)
    for shift, places in shifts.items():
        turned = pltpu.roll(value, shift, len(value.shape) - 1) if shift else value
        chosen = place == places[0]
        for other in places[1:]:
            chosen = jnp.logical_or(chosen, place == other)
        result = jnp.where(chosen, turned, result)
    return result


def pair_kernel(
    own_count, extent, width, pad, listed, total, own, far, plane_even, plane_odd, back_even,
    back_odd, first_block, scale,
    own_out, far_out, boxes, sums, density_a, density_b, middle, field_a, field_b,
):
    plane = (plane_even, plane_odd)
    chunks = width // lanes
    half = chunks // 2
    side = width // 2
    tall = extent + 2 * pad
    dead = boxes.shape[0] - 1
    inner = slice(pad, pad + extent)
    zeros = jnp.zeros((chunks, tall, lanes), jnp.float32)
    edge = jnp.zeros((chunks, pad, lanes), jnp.float32)

    def part(s):
        return slice(s * lanes, (s + 1) * lanes)

    def put(n, at, rows, read):
        for s in range(half):
            boxes[n, s, at : at + rows] = read(part(s)).astype(jnp.float32)
            boxes[n, half + s, at : at + rows] = mirrored(
                read(part(chunks - 1 - s)).astype(jnp.float32), extent
            )

    def clear(n, carry):
        boxes[n, :, :pad] = edge
        boxes[n, :, pad + extent :] = edge
        sums[n] = zeros
        return carry

    def fill_own(n, carry):
        put(n, pad, extent, lambda columns: own[n, :, columns])
        return carry

    def fill_far(n, carry):
        group_size, per, rows = far.shape[1:4]
        for h in range(group_size):
            put(
                own_count + n, pad + h * rows, rows,
                lambda columns: far[n // per, h, n % per, :, columns],
            )
        return carry

    lax.fori_loop(0, dead, clear, 0)
    lax.fori_loop(0, own_count, fill_own, 0)
    lax.fori_loop(0, dead - own_count, fill_far, 0)
    boxes[dead] = zeros
    sums[dead] = zeros
    field_b[...] = jnp.zeros_like(field_b)

    def unpack(turn, b):
        word = listed[(turn + 1) * batch + b]
        return word % 256, (word // 256) % 256, 2 * pad - word // 65536

    def products(turn, density, b):
        first, second, start = unpack(turn, b)
        rows = slice(b * extent, (b + 1) * extent)
        window = pl.ds(start, extent)
        for s in range(half):
            low = boxes[first, s, inner] * boxes[second, s, window, :]
            high = boxes[first, half + s, inner] * boxes[second, half + s, window, :]
            density[rows, part(s)] = (low + high).astype(jnp.bfloat16)
            density[rows, part(half + s)] = (low - high).astype(jnp.bfloat16)

    def terms(turn, field, b):
        first, second, start = unpack(turn, b)
        rows = slice(b * extent, (b + 1) * extent)
        window = pl.ds(start, extent)
        some = 4
        for q in range(0, chunks, some):
            group = range(q, q + some)
            values = [field[rows, part(s)] for s in group]
            adds = [values[k] * boxes[second, s, window, :] for k, s in enumerate(group)]
            were = [sums[first, s, inner] for s in group]
            for k, s in enumerate(group):
                sums[first, s, inner] = were[k] + adds[k]
            adds = [values[k] * boxes[first, s, inner] for k, s in enumerate(group)]
            were = [sums[second, s, window, :] for s in group]
            for k, s in enumerate(group):
                sums[second, s, window, :] = were[k] + adds[k]

    step = 256

    def forward(density, h, n):
        columns = slice(n * step, (n + 1) * step)
        target = slice(h * side + n * step, h * side + (n + 1) * step)
        wave = jnp.dot(
            density[:, h * side : (h + 1) * side], plane[h][:, columns],
            preferred_element_type=jnp.float32,
        )
        wave = jnp.dot(
            first_block[...], wave.astype(jnp.bfloat16), preferred_element_type=jnp.float32
        )
        wave = wave.reshape(batch, extent, step) * scale[:, target][None]
        wave = wave.reshape(batch * extent, step).astype(jnp.bfloat16)
        wave = jnp.dot(first_block[...], wave, preferred_element_type=jnp.float32)
        middle[:, target] = wave.astype(jnp.bfloat16)

    def backward(field, n):
        columns = slice(n * step, (n + 1) * step)
        even = jnp.dot(middle[:, :side], back_even[:, columns], preferred_element_type=jnp.float32)
        odd = jnp.dot(middle[:, side:], back_odd[:, columns], preferred_element_type=jnp.float32)
        field[:, columns] = even + odd
        field[:, side + n * step : side + (n + 1) * step] = even - odd

    def phase(turn, density, field, next_density, last_field):
        steps = [
            functools.partial(forward, density, h, n) for h in range(2) for n in range(side // step)
        ] + [functools.partial(backward, field, n) for n in range(side // step)]
        asides = []
        for b in range(batch):
            asides.append(functools.partial(terms, turn - 1, last_field, b))
            asides.append(functools.partial(products, turn + 1, next_density, b))
        done = 0
        for k, work in enumerate(steps):
            work()
            upto = len(asides) * (k + 1) // len(steps)
            for aside in asides[done:upto]:
                aside()
            done = upto

    for b in range(batch):
        products(0, density_a, b)

    def double_turn(i, carry):
        phase(2 * i, density_a, field_a, density_b, field_b)
        phase(2 * i + 1, density_b, field_b, density_a, field_a)
        return carry

    turns = (total[0] + 2 * batch - 1) // (2 * batch)
    lax.fori_loop(0, turns, double_turn, 0)
    for b in range(batch):
        terms(2 * turns - 1, field_b, b)

    def give_own(n, carry):
        for s in range(half):
            own_out[n, :, part(s)] = sums[n, s, inner].astype(own_out.dtype)
            own_out[n, :, part(chunks - 1 - s)] = mirrored(sums[n, half + s, inner], extent).astype(
                own_out.dtype
            )
        return carry

    def give_far(n, carry):
        group_size, per, rows = far_out.shape[1:4]
        for h in range(group_size):
            block = slice(pad + h * rows, pad + (h + 1) * rows)
            for s in range(half):
                far_out[n // per, h, n % per, :, part(s)] = sums[own_count + n, s, block].astype(
                    far_out.dtype
                )
                far_out[n // per, h, n % per, :, part(chunks - 1 - s)] = mirrored(
                    sums[own_count + n, half + s, block], extent
                ).astype(far_out.dtype)
        return carry

    lax.fori_loop(0, own_count, give_own, 0)
    lax.fori_loop(0, dead - own_count, give_far, 0)


def join_kernel(local, own, returned, out):
    out[...] = own[...].astype(jnp.float32)

    def add(n, carry):
        out[local[n]] += returned[n].astype(jnp.float32)
        return carry

    lax.fori_loop(0, returned.shape[0], add, 0)


def shards(orbitals, anchors, wanted, pairs, counts):
    group_size = lax.axis_size("grp")
    member = lax.axis_index("orb")
    position = lax.axis_index("grp")
    own_count, rows, width = orbitals.shape
    extent = rows * group_size
    pad = extent // 4
    owners, per_owner = wanted.shape[0], wanted.shape[2]
    per = -(-per_owner // group_size)
    slots = owners * per
    capacity = pairs.shape[2]
    smem = pl.BlockSpec(memory_space=pltpu.SMEM)
    vmem = pl.BlockSpec(memory_space=pltpu.VMEM)

    slab = orbitals.astype(jnp.bfloat16)
    own_full = lax.all_gather(slab, "grp", axis=1, tiled=True)

    send_ids = lax.dynamic_index_in_dim(wanted, member, 1, keepdims=False)
    request = lax.dynamic_index_in_dim(wanted, member, 0, keepdims=False).reshape(-1)
    if group_size <= per_owner:
        room = per * group_size - per_owner
        send_ids = jnp.pad(send_ids, ((0, 0), (0, room)), constant_values=-1)
    else:
        send_ids = jnp.tile(send_ids, (1, -(-group_size // per_owner)))[:, :group_size]
    send_ids = send_ids.reshape(-1)
    send_local = jnp.where(send_ids >= 0, send_ids - member * own_count, 0)
    outgoing = slab[send_local]
    arrived = lax.all_to_all(outgoing, ("orb", "grp"), split_axis=0, concat_axis=0, tiled=True)
    arrived = arrived.reshape(owners, group_size, per, rows, width)

    sine_rows = sine_table(extent)
    middle = extent // 2
    plane = [jnp.kron(sine_rows[:middle, k::2], sine_rows) for k in range(2)]
    back = [jnp.kron(sine_rows[k::2, :middle], sine_rows) for k in range(2)]
    first_block = jnp.kron(jnp.eye(batch, dtype=jnp.bfloat16), sine_rows)
    divisor = denominator(extent)
    divisor = jnp.concatenate([divisor[:, 0::2], divisor[:, 1::2]], axis=1)
    scale = (1.0 / divisor).reshape(extent, width)

    size = group_size * capacity + 5 * batch
    sizes = (group_size, capacity, own_count, per_owner, per, slots, pad)
    words = jax.ShapeDtypeStruct((size,), jnp.int32)
    listed, total = pl.pallas_call(
        functools.partial(list_kernel, sizes),
        out_shape=(words, jax.ShapeDtypeStruct((1,), jnp.int32)),
        in_specs=[smem] * 5,
        out_specs=(smem, smem),
        scratch_shapes=[pltpu.SMEM((size,), jnp.int32), pltpu.SMEM((group_size,), jnp.int32)],
    )(
        jnp.stack([member, position]).astype(jnp.int32),
        pairs.reshape(-1),
        counts.reshape(-1),
        anchors,
        request,
    )

    tall = extent + 2 * pad
    chunks = width // lanes

    kept = own_count + slots + 1
    own_sum, far_sum = pl.pallas_call(
        functools.partial(pair_kernel, own_count, extent, width, pad),
        out_shape=(
            jax.ShapeDtypeStruct((own_count, extent, width), jnp.bfloat16),
            jax.ShapeDtypeStruct(arrived.shape, jnp.bfloat16),
        ),
        in_specs=[smem, smem] + [vmem] * 8,
        out_specs=(vmem, vmem),
        scratch_shapes=[
            pltpu.VMEM((kept, chunks, tall, lanes), jnp.float32),
            pltpu.VMEM((kept, chunks, tall, lanes), jnp.float32),
            pltpu.VMEM((batch * extent, width), jnp.bfloat16),
            pltpu.VMEM((batch * extent, width), jnp.bfloat16),
            pltpu.VMEM((batch * extent, width), jnp.bfloat16),
            pltpu.VMEM((batch * extent, width), jnp.float32),
            pltpu.VMEM((batch * extent, width), jnp.float32),
        ],
        cost_estimate=pl.CostEstimate(
            flops=60_000_000_000, bytes_accessed=16_000_000, transcendentals=0
        ),
        compiler_params=pltpu.CompilerParams(vmem_limit_bytes=54 * 2**20),
    )(listed, total, own_full, arrived, *plane, *back, first_block, scale)
    returned = lax.all_to_all(
        far_sum.reshape(-1, rows, width), ("orb", "grp"), split_axis=0, concat_axis=0, tiled=True
    )
    own_mine = lax.psum_scatter(own_sum, "grp", scatter_dimension=1, tiled=True)
    return pl.pallas_call(
        join_kernel,
        out_shape=jax.ShapeDtypeStruct((own_count, rows, width), jnp.float32),
        in_specs=[smem, vmem, vmem],
        out_specs=vmem,
        compiler_params=pltpu.CompilerParams(vmem_limit_bytes=40 * 2**20),
    )(send_local, own_mine, returned)


def solution(mesh):
    return jax.shard_map(
        shards,
        mesh=mesh,
        in_specs=(P("orb", "grp", None), P(), P(), P("orb", None, None, None), P("orb", None)),
        out_specs=P("orb", "grp", None),
        check_vma=False,
    )
```
